512 devices in a mesh: dp: 8 (over y), expert: 64 (over x, z, core).
Axes of the slice: x: 4, y: 8, z: 8, core: 2. Of those that a mesh axis runs over, the one named last changes fastest.
Arguments:
- tokens: bfloat16 [65536, 4096], P(('dp', 'expert'))
- routes: int32 [65536, 8], P(('dp', 'expert')), may hold values from 0 to 127, as said below
- old_slots: int32 [64], replicated, may hold values from 0 to 63, each once
- new_slots: int32 [64], replicated, may hold values from 0 to 63, each once
- weights: bfloat16 [64, 1536, 4096], P('expert', None, 'dp'), may hold values from -6 to 6
- patterns: int32 [64, 1536, 32], P('expert'), may hold values from 0 to 5
- inverse: float32 [64, 128, 128], P('expert'), as said below
Outputs:
- new_weights: bfloat16 [64, 1536, 4096], P('expert', None, 'dp')
The draws below stay inside these ranges and needn't reach their ends.
Inputs may be any that keep to these rules, and one draw needn't show every extreme that they name: `routes`: each row names 8 distinct experts; within the 128 rows of one device no expert is named by more than 9 rows, and some expert below 64 is named by exactly 9 rows of every device. `old_slots`: each of 0 to 63 once. `new_slots`: each of 0 to 63 once. `inverse`: symmetric.
All inputs are finite; a program needn't handle non-finite values.
Results may differ from the reference program's by a relative error of at most 0.001.
Values may be sent and summed in bfloat16 or wider, within the bound.
No kernel may reach another device: no remote copies, remote signals or barrier semaphores. Data moves between devices by JAX's collectives and lax.ppermute only.
A program may use at most 64 MiB of HBM per device.

```python
import jax
import jax.numpy as jnp
import numpy as np
from jax import lax

D = 4096
FF = 1536
ROUTED = 128
TOPK = 8
PANEL = 128
CAP = 9
TOK_DEV = 128
EXPERTS = 64
TOKENS = 65536


def draw_tokens(key, part):
    key = jax.random.fold_in(key, 11)
    base_key, row_key, column_key = jax.random.split(key, 3)
    position = jnp.arange(TOKENS, dtype=jnp.float32) / TOKENS
    base = jnp.clip(jax.random.normal(base_key, (TOKENS, D), jnp.float32), -5.0, 5.0)
    trend = 3.0 ** position
    row_scale = trend * 3.0 ** jax.random.uniform(row_key, (TOKENS,), jnp.float32) / 3.0
    column_scale = 10.0 ** jax.random.uniform(column_key, (D,), jnp.float32) / 3.0
    return (base * row_scale[:, None] * column_scale[None, :]).astype(jnp.bfloat16)


def draw_routes(key, part):
    key = jax.random.fold_in(key, 23)
    pinned_key, busy_key, block_key = jax.random.split(key, 3)
    pinned = jax.random.randint(pinned_key, (), 0, EXPERTS)
    busy = jax.random.randint(busy_key, (ROUTED,), 0, 4)
    pool_size = ROUTED * CAP
    expert_ids = jnp.repeat(jnp.arange(ROUTED, dtype=jnp.int32), CAP)
    copies = jnp.tile(jnp.arange(CAP, dtype=jnp.int32), ROUTED)

    def one_block(block_seed):
        score_key, order_key = jax.random.split(block_seed)
        scores = jax.random.randint(score_key, (pool_size,), 0, 48) + 6 * copies - 12 * busy[expert_ids]
        scores = jnp.where(expert_ids == pinned, -1000, scores)
        ranks = scores * pool_size + jax.random.permutation(order_key, pool_size)
        ordering = jnp.argsort(ranks, stable=True)
        picked = jnp.sort(expert_ids[ordering[:TOK_DEV * TOPK]])
        return picked.reshape(TOPK, TOK_DEV).T
    seeds = jax.random.split(block_key, TOKENS // TOK_DEV)
    result = jax.vmap(one_block)(seeds)
    return result.reshape(TOKENS, TOPK).astype(jnp.int32)


def draw_inverse(key, part):
    key = jax.random.fold_in(key, 37)
    noise_key, diag_key = jax.random.split(key)
    noise = jax.random.normal(noise_key, (EXPERTS, PANEL, PANEL), jnp.float32)
    symmetric = 0.035 * (noise + jnp.swapaxes(noise, 1, 2))
    leading = 0.5 + jax.random.uniform(diag_key, (EXPERTS, PANEL), jnp.float32)
    return symmetric + leading[:, :, None] * jnp.eye(PANEL, dtype=jnp.float32)[None]


def touch_ends(values, stream_key, low, largest):
    longest = values.shape.index(max(values.shape))
    spots = []
    for shift in (0, 1):
        where = [jax.random.randint(jax.random.fold_in(stream_key, axis), (), 0, length) for axis, length in enumerate(values.shape)]
        where[longest] = (where[longest] + shift) % values.shape[longest]
        spots.append(tuple(where))
    return values.at[spots[0]].set(low).at[spots[1]].set(largest)


def levels(stream_key, dims, shards, smallest, top_value):
    def one(axis_at, parts):
        steps = jax.random.uniform(jax.random.fold_in(jax.random.fold_in(stream_key, 6), axis_at), (parts,), jnp.float32, smallest / len(shards), top_value / len(shards))
        return jnp.repeat(jnp.exp(steps), dims[axis_at] // parts).reshape((-1,) + (1,) * (len(dims) - axis_at - 1))

    loudness = one(*shards[0])
    for cut in shards[1:]:
        loudness = loudness * one(*cut)
    return loudness


def normal_values(own_key, dims, spread, reach, cuts=(), held_as=jnp.bfloat16):
    values = spread * jax.random.normal(own_key, dims, jnp.float32)
    if cuts:
        values = values * levels(own_key, dims, cuts, -0.22, 0.18)
    return jnp.clip(values, -reach, reach).astype(held_as)


def setup_inputs(seed: int = 0) -> dict:
    key_of = jax.random.split(jax.random.key(seed), 8)
    return {
        "tokens": draw_tokens(jax.random.fold_in(key_of[7], 71), 0),
        "routes": draw_routes(jax.random.fold_in(key_of[7], 71), 0),
        "old_slots": jax.random.permutation(key_of[2], EXPERTS).astype(jnp.int32),
        "new_slots": jax.random.permutation(key_of[3], EXPERTS).astype(jnp.int32),
        "weights": normal_values(key_of[4], (EXPERTS, FF, D), 1.0, 6.0, ((0, 64), (2, 8))),
        "patterns": touch_ends(jax.random.randint(key_of[5], (EXPERTS, FF, PANEL // 4), 0, 6), jax.random.fold_in(key_of[5], 1), 0, 5).astype(jnp.int32),
        "inverse": draw_inverse(jax.random.fold_in(key_of[7], 71), 0),
    }


KEEP_PAIRS = np.array([[1, 1, 0, 0], [1, 0, 1, 0], [1, 0, 0, 1], [0, 1, 1, 0], [0, 1, 0, 1], [0, 0, 1, 1]])
EPSILON = 1e-6
DAMPING = 0.01


def mask_from(pattern):
    onehot = (pattern[..., None] == jnp.arange(6, dtype=jnp.int32)).astype(jnp.float32)
    table = jnp.asarray(KEEP_PAIRS, dtype=jnp.float32)
    picked = jnp.sum(onehot[..., :, None] * table, axis=-2)
    return picked.reshape(pattern.shape[0], -1)


def slot_rows(block_routes, wanted, capacity):
    count_rows = block_routes.shape[0]
    matched = jnp.any(block_routes[:, :, None] == wanted[None, None, :], axis=1).astype(jnp.int32)
    ranked = jnp.cumsum(matched, axis=0, dtype=jnp.int32) - 1
    places = jnp.arange(capacity, dtype=jnp.int32)
    chosen = (matched.T[:, None, :] == 1) & (ranked.T[:, None, :] == places[None, :, None])
    row_ids = jnp.arange(count_rows, dtype=jnp.int32)
    indices = jnp.sum(jnp.where(chosen, row_ids[None, None, :], 0), axis=-1).astype(jnp.int32)
    filled = jnp.any(chosen, axis=-1)
    return indices, filled


def panel_solve(panel_held, mask, gram_panel, inverse_block):
    panel_part = panel_held.astype(jnp.float32)
    dropped = (1.0 - mask) * panel_part
    damped = gram_panel + DAMPING * jnp.eye(PANEL, dtype=jnp.float32)
    step_one = jnp.dot(dropped, damped, precision=lax.Precision.HIGHEST)
    refitted = mask * (panel_part + jnp.dot(step_one, inverse_block, precision=lax.Precision.HIGHEST))
    return refitted, refitted - panel_part


def reference(tokens, routes, old_slots, new_slots, weights, patterns, inverse):
    blocks = tokens.reshape(-1, TOK_DEV, D)
    route_blocks = routes.reshape(-1, TOK_DEV, TOPK)

    def refit_slot(slot_index):
        expert_id = old_slots[slot_index]
        indices, filled = jax.vmap(lambda block_routes: slot_rows(block_routes, expert_id[None], CAP))(route_blocks)
        gathered = jnp.take_along_axis(blocks, indices[:, 0, :, None], axis=1)
        gathered = jnp.where(filled[:, 0, :, None], gathered, 0).astype(jnp.float32).reshape(-1, D)
        gram_full = jnp.dot(gathered.T, gathered[:, :PANEL], precision=lax.Precision.HIGHEST)
        squares = jnp.sum(gathered * gathered, axis=0)
        scaling = jnp.mean(squares) + EPSILON
        normed = gram_full / scaling
        normed_diag = squares / scaling
        held = weights[slot_index]
        refitted, change = panel_solve(held[:, :PANEL], mask_from(patterns[slot_index]), normed[:PANEL], inverse[slot_index])
        adjusted = held.astype(jnp.float32) - jnp.dot(change, normed.T, precision=lax.Precision.HIGHEST) / (normed_diag + DAMPING)[None, :]
        adjusted = jnp.concatenate([refitted, adjusted[:, PANEL:]], axis=1)
        return adjusted.astype(jnp.bfloat16)

    refit_all = lax.map(refit_slot, jnp.arange(EXPERTS, dtype=jnp.int32))
    slot_ids = jnp.arange(EXPERTS, dtype=jnp.int32)
    source_slot = jnp.sum(jnp.where(old_slots[None, :] == new_slots[:, None], slot_ids[None, :], 0), axis=1).astype(jnp.int32)
    return jnp.take(refit_all, source_slot, axis=0)
```

```python
import jax
import jax.numpy as jnp
from jax import lax
from jax.experimental import pallas as pl
from jax.experimental.pallas import tpu as pltpu
from jax.sharding import Mesh
from jax.sharding import PartitionSpec as P

D = 4096
FF = 1536
PANEL = 128
EPSILON = 1e-06
DAMPING = 0.01
NY, NX, NZ, NC = 8, 4, 8, 2
HELD = 32
ROWS = 168
EXPERT = ("x", "z", "c")
bf16 = jnp.bfloat16
f32 = jnp.float32
HIGHEST = lax.Precision.HIGHEST
VMEM = pl.BlockSpec(memory_space=pltpu.VMEM)
SMEM = pl.BlockSpec(memory_space=pltpu.SMEM)


def prep_kernel(tokens, routes, patterns, inverse, blocks, panel, extra):
    squares = jnp.zeros((128, 128), f32)
    for s in range(32):
        part = tokens[:, s * 128 : (s + 1) * 128]
        blocks[s] = part
        wide = part.astype(f32)
        squares = squares + wide * wide
    panel[0:128, :] = tokens[:, 0:128].astype(f32).T.astype(bf16)
    norms = jnp.sum(squares.T, axis=0, keepdims=True) * (1.0 / D)
    high = norms.astype(bf16).astype(f32)
    named = jnp.concatenate(
        [routes[...].astype(f32), jnp.zeros((128, 120), f32)], axis=1
    ).T
    panel[128:144, :] = jnp.concatenate(
        [named[0:8], high, norms - high, jnp.zeros((6, 128), f32)], axis=0
    ).astype(bf16)
    numbers = patterns[...].astype(f32)
    extra[0:48, :] = jnp.concatenate(
        [numbers[48 * q : 48 * (q + 1)] for q in range(4)], axis=1
    ).astype(bf16)
    rest = inverse[...]
    for q in range(3):
        piece = rest.astype(bf16)
        extra[48 + 16 * q : 64 + 16 * q, :] = piece
        rest = rest - piece.astype(f32)
    extra[96:128, :] = jnp.zeros((32, 128), bf16)


def prepare(tokens, routes, patterns, inverse):
    return pl.pallas_call(
        prep_kernel,
        out_shape=(
            jax.ShapeDtypeStruct((32, 128, 128), bf16),
            jax.ShapeDtypeStruct((144, 128), bf16),
            jax.ShapeDtypeStruct((128, 128), bf16),
        ),
        in_specs=[VMEM] * 4,
        out_specs=(VMEM,) * 3,
        compiler_params=pltpu.CompilerParams(vmem_limit_bytes=16 * 1024 * 1024),
    )(tokens, routes, patterns, inverse)


def gram_kernel(where, wanted, own, other, panels, out, left_all, right, squares, marks, left, total, norms):
    x, c = where[0], where[1]
    ids = wanted[...]
    norms[...] = jnp.zeros_like(norms)
    for half, source in ((0, own), (1, other)):
        core = c if half == 0 else 1 - c

        @pl.loop(0, HELD)
        def _(b):
            place = ((b % NX) * NC + core) * NY + b // NX
            at = pl.ds(pl.multiple_of((half * HELD + b) * 128, 128), 128)
            turned = panels[place, 0:128, :]
            notes = panels[place, 128:144, :].astype(f32)
            left_all[:, at] = turned
            right[at, 128:256] = turned.astype(f32).T.astype(bf16)
            part = source[b]
            right[at, 0:128] = part
            wide = part.astype(f32)
            wide = wide * wide
            high = wide.astype(bf16)
            squares[at, 0:128] = high
            squares[at, 128:256] = (wide - high.astype(f32)).astype(bf16)
            hit = jnp.zeros((HELD, 128), f32)
            for k in range(8):
                hit = jnp.where(notes[k : k + 1, :] == ids, 1.0, hit)
            marks[:, at] = hit
            norms[...] += hit * (notes[8:9, :] + notes[9:10, :])

    chunk = 2048

    @pl.loop(0, 4)
    def _(g):
        @pl.loop(0, 4)
        def _(k):
            at = pl.ds(pl.multiple_of(k * chunk, chunk), chunk)
            hits = marks[pl.ds(pl.multiple_of(g * 8, 8), 8), at]
            for j in range(8):
                row = jnp.broadcast_to(hits[j : j + 1, :], (16, chunk)).astype(bf16)
                for r in range(8):
                    left[j * 128 + r * 16 : j * 128 + r * 16 + 16, :] = (
                        left_all[r * 16 : r * 16 + 16, at] * row
                    )
            product = jnp.dot(left[...], right[at, :], preferred_element_type=f32)

            @pl.when(k == 0)
            def _():
                total[...] = product

            @pl.when(k > 0)
            def _():
                total[...] += product

        for j in range(8):
            out[g * 8 + j, 0:128, :] = total[j * 128 : (j + 1) * 128, 0:128]
            quarter = pl.ds(pl.multiple_of(j * 128 + 32 * x, 32), 32)
            out[g * 8 + j, 128:160, :] = total[quarter, 128:256]

    sums = jnp.dot(marks[...].astype(bf16), squares[...], preferred_element_type=f32)
    sums = sums[:, 0:128] + sums[:, 128:256]
    scale = jnp.broadcast_to(jnp.sum(norms[...], axis=1, keepdims=True), (HELD, 128))
    for e in range(HELD):
        out[e, 160:168, :] = jnp.concatenate(
            [sums[e : e + 1], scale[e : e + 1], jnp.zeros((6, 128), f32)], axis=0
        )


def gram(where, wanted, own, other, panels):
    return pl.pallas_call(
        gram_kernel,
        out_shape=jax.ShapeDtypeStruct((HELD, ROWS, 128), f32),
        in_specs=[SMEM] + [VMEM] * 4,
        out_specs=VMEM,
        scratch_shapes=[
            pltpu.VMEM((128, 8192), bf16),
            pltpu.VMEM((8192, 256), bf16),
            pltpu.VMEM((8192, 256), bf16),
            pltpu.VMEM((HELD, 8192), f32),
            pltpu.VMEM((1024, 2048), bf16),
            pltpu.VMEM((1024, 256), f32),
            pltpu.VMEM((HELD, 128), f32),
        ],
        compiler_params=pltpu.CompilerParams(vmem_limit_bytes=48 * 1024 * 1024),
        cost_estimate=pl.CostEstimate(
            flops=2 * 4096 * 8192 * 256, bytes_accessed=8 << 20, transcendentals=0
        ),
    )(where, wanted, own, other, panels)


def refit_kernel(where, sums, shared, held, out, normed, scaled, inverse):
    y = where[2]
    scaling = sums[0, 161:162, :] + EPSILON
    for q in range(NX):
        diagonal = sums[q, 160:161, :] / scaling + DAMPING
        scaled[:, q * 128 : (q + 1) * 128] = sums[q, 0:128, :] / scaling / diagonal
        normed[q * 32 : (q + 1) * 32, :] = sums[q, 128:160, :] / scaling
    a = lax.broadcasted_iota(jnp.int32, (128, 128), 0)
    b = lax.broadcasted_iota(jnp.int32, (128, 128), 1)
    normed[...] += jnp.where(a == b, DAMPING, 0.0)
    for q in range(NY):
        inverse[q * 16 : (q + 1) * 16, :] = (
            shared[q, 240:256, :].astype(f32)
            + shared[q, 256:272, :].astype(f32)
            + shared[q, 272:288, :].astype(f32)
        )

    @pl.loop(0, NY)
    def _(q):
        numbers = shared[q, 192:240, :]
        spread = []
        for part in range(4):
            pick = jnp.where(a == part * 32 + b // 4, 1.0, 0.0).astype(bf16)
            spread.append(jnp.dot(numbers, pick, preferred_element_type=f32))
        number = jnp.concatenate(spread, axis=0)
        lane = lax.broadcasted_iota(jnp.int32, (192, 128), 1) % 4
        code = number.astype(jnp.int32)
        kept = jnp.where(lane == 0, 0b000111, jnp.where(lane == 1, 0b011001, jnp.where(lane == 2, 0b101010, 0b110100)))
        mask = ((kept >> code) & 1).astype(f32)
        panel = shared[q, 0:192, :].astype(f32)
        dropped = (1.0 - mask) * panel
        step = jnp.dot(dropped, normed[...], precision=HIGHEST, preferred_element_type=f32)
        step = jnp.dot(step, inverse[...], precision=HIGHEST, preferred_element_type=f32)
        refitted = mask * (panel + step)
        change = refitted - panel
        correction = jnp.dot(change, scaled[...], precision=HIGHEST, preferred_element_type=f32)
        rows = pl.ds(pl.multiple_of(q * 192, 64), 192)
        for k in range(4):
            for half in range(2):
                piece = held[16 * k + 2 * q + half, 0:96, :].astype(f32)
                fixed = piece - correction[half * 96 : (half + 1) * 96, k * 128 : (k + 1) * 128]
                out[pl.ds(pl.multiple_of(q * 192 + half * 96, 32), 96), k * 128 : (k + 1) * 128] = fixed.astype(bf16)

        @pl.when(y == 0)
        def _():
            out[rows, 0:128] = refitted.astype(bf16)


def refit(where, sums, shared, held):
    return pl.pallas_call(
        refit_kernel,
        out_shape=jax.ShapeDtypeStruct((FF, 512), bf16),
        in_specs=[SMEM] + [VMEM] * 3,
        out_specs=VMEM,
        scratch_shapes=[
            pltpu.VMEM((128, 128), f32),
            pltpu.VMEM((128, 512), f32),
            pltpu.VMEM((128, 128), f32),
        ],
        compiler_params=pltpu.CompilerParams(vmem_limit_bytes=32 * 1024 * 1024),
    )(where, sums, shared, held)


def swap(value, axis, size, step):
    return lax.ppermute(value, axis, [(i, (i + step) % size) for i in range(size)])


def after(value, *others):
    return lax.optimization_barrier((value, *others))[0]


def shards(tokens, routes, old_slots, new_slots, weights, patterns, inverse):
    x, y, z, c = (lax.axis_index(name) for name in ("x", "y", "z", "c"))
    me = (x * NZ + z) * NC + c
    where = jnp.stack([x, c, y]).astype(jnp.int32)
    slot = jnp.arange(64, dtype=jnp.int32)
    source = jnp.sum(jnp.where(old_slots[None, :] == new_slots[:, None], slot[None, :], 0), axis=1)
    order = new_slots.reshape(NX, NZ, NC).transpose(2, 1, 0).reshape(NC, HELD)
    wanted = jnp.broadcast_to(
        lax.dynamic_index_in_dim(order, c, 0, keepdims=False)[:, None], (HELD, 128)
    ).astype(f32)

    blocks, panel, extra = prepare(
        tokens,
        routes,
        lax.dynamic_slice_in_dim(patterns[0], y * 192, 192, 0),
        lax.dynamic_slice_in_dim(inverse[0], y * 16, 16, 0),
    )
    panels = lax.all_gather(panel, "y", axis=0, tiled=False)
    panels = lax.all_gather(panels, ("x", "c"), axis=0, tiled=False).reshape(64, 144, 128)
    own = lax.all_to_all(blocks, ("y", "x"), 0, 0, tiled=True)
    other = swap(own, "c", NC, 1)

    pieces = weights[0].reshape(16, 96, 4, 128).transpose(2, 0, 1, 3).reshape(64, 96, 128)
    tail = jnp.pad(extra.reshape(64, 2, 128), ((0, 0), (0, 6), (0, 0)))
    pieces = jnp.concatenate([pieces, tail], axis=1)
    pieces = after(pieces, own)
    spread = lax.all_to_all(pieces, EXPERT, 0, 0, tiled=True)
    spread = jnp.take(spread, source, axis=0, mode="clip")
    held = lax.all_to_all(spread, EXPERT, 0, 0, tiled=True)

    sums = gram(where, wanted, own, other, panels)
    sums = lax.psum_scatter(sums, "z", scatter_dimension=0, tiled=True)
    sums = lax.all_to_all(sums, "x", 0, 0, tiled=True)

    moved = held[0:16, 0:96].reshape(NY, 192, 128)
    moved = lax.all_to_all(moved, "y", 0, 0, tiled=True)[0]
    shared = jnp.concatenate([moved, held[:, 96:98].reshape(128, 128)[0:96]], axis=0)
    shared = lax.all_gather(shared, "y", axis=0, tiled=False)
    return refit(where, sums, shared, held)[None]


def solution(mesh):
    grid = Mesh(mesh.devices.reshape(NY, NX, NZ, NC), ("y", "x", "z", "c"))
    placed = (
        P(("y", "x", "z", "c"), None),
        P(("y", "x", "z", "c"), None),
        P(),
        P(),
        P(EXPERT, None, "y"),
        P(EXPERT, None, None),
        P(EXPERT, None, None),
    )
    return jax.shard_map(
        shards, mesh=grid, in_specs=placed, out_specs=P(EXPERT, None, "y"), check_vma=False
    )
```

```python
import jax
import jax.numpy as jnp
from jax import lax
from jax.experimental import pallas as pl
from jax.experimental.pallas import tpu as pltpu
from jax.sharding import Mesh
from jax.sharding import PartitionSpec as P

D = 4096
FF = 1536
PANEL = 128
EPSILON = 1e-06
DAMPING = 0.01
NY, NX, NZ, NC = 8, 4, 8, 2
HELD = 32
ROWS = 168
EXPERT = ("x", "z", "c")
bf16 = jnp.bfloat16
f32 = jnp.float32
VMEM = pl.BlockSpec(memory_space=pltpu.VMEM)
SMEM = pl.BlockSpec(memory_space=pltpu.SMEM)


def sort_kernel(where, *refs):
    came, (panels, rows) = refs[:NY], refs[NY:]
    for s in range(NY):
        panels[s * 144 : (s + 1) * 144, :] = came[s][0:144, :]

        @pl.when(where[2] == s)
        def _(s=s):
            rows[...] = came[s][144:336, :].astype(f32)


def sort(where, came):
    return pl.pallas_call(
        sort_kernel,
        out_shape=(
            jax.ShapeDtypeStruct((NY * 144, 128), bf16),
            jax.ShapeDtypeStruct((192, 128), f32),
        ),
        in_specs=[SMEM] + [VMEM] * NY,
        out_specs=(VMEM,) * 2,
        compiler_params=pltpu.CompilerParams(vmem_limit_bytes=16 * 1024 * 1024),
    )(where, *came)


def pack_kernel(weights, patterns, inverse, rows, pieces):
    numbers = patterns[...].astype(f32)
    rest = inverse[...]
    parts = []
    for q in range(3):
        piece = rest.astype(bf16).astype(f32)
        parts.append(piece)
        rest = rest - piece
    extra = jnp.concatenate(
        [numbers[48 * q : 48 * (q + 1)] for q in range(4)], axis=1
    )
    extra = jnp.concatenate([extra] + parts + [jnp.zeros((32, 128), f32)], axis=0)
    for p in range(64):
        k, q = p // 16, p % 16
        pieces[p, 0:96, :] = weights[96 * q : 96 * (q + 1), 128 * k : 128 * (k + 1)]
        pieces[p, 96:104, :] = jnp.concatenate(
            [extra[2 * p : 2 * p + 2], rows[3 * p : 3 * p + 3, :], jnp.zeros((3, 128), f32)], axis=0
        ).astype(bf16)


def pack(weights, patterns, inverse, rows):
    return pl.pallas_call(
        pack_kernel,
        out_shape=jax.ShapeDtypeStruct((64, 104, 128), bf16),
        in_specs=[VMEM] * 4,
        out_specs=VMEM,
        compiler_params=pltpu.CompilerParams(vmem_limit_bytes=16 * 1024 * 1024),
    )(weights, patterns, inverse, rows)


def prep_kernel(tokens, routes, rows, blocks, notes):
    squares = jnp.zeros((128, 128), f32)
    for s in range(32):
        part = tokens[:, s * 128 : (s + 1) * 128]
        blocks[s] = part
        wide = part.astype(f32)
        squares = squares + wide * wide
    turned = tokens[:, 0:128].astype(f32).T.astype(bf16)
    norms = jnp.sum(squares.T, axis=0, keepdims=True) * (1.0 / D)
    high = norms.astype(bf16).astype(f32)
    named = jnp.concatenate(
        [routes[...].astype(f32), jnp.zeros((128, 120), f32)], axis=1
    ).T
    facts = jnp.concatenate(
        [named[0:8], high, norms - high, jnp.zeros((6, 128), f32)], axis=0
    ).astype(bf16)
    for s in range(NY):
        notes[s, 0:128, :] = turned
        notes[s, 128:144, :] = facts
        notes[s, 144:336, :] = rows[s * 192 : (s + 1) * 192, :]


def prepare(tokens, routes, rows):
    return pl.pallas_call(
        prep_kernel,
        out_shape=(
            jax.ShapeDtypeStruct((32, 128, 128), bf16),
            jax.ShapeDtypeStruct((NY, 336, 128), bf16),
        ),
        in_specs=[VMEM] * 3,
        out_specs=(VMEM,) * 2,
        compiler_params=pltpu.CompilerParams(vmem_limit_bytes=16 * 1024 * 1024),
    )(tokens, routes, rows)


def gram_kernel(where, wanted, own, other, panels, out, left_all, right, squares, marks, left, total, norms):
    x, c, y = where[0], where[1], where[2]
    ids = wanted[...]
    norms[...] = jnp.zeros_like(norms)
    for half, source in ((0, own), (1, other)):
        core = c if half == 0 else 1 - c

        @pl.loop(0, HELD)
        def _(b):
            place = ((b % NX) * NC + core) * NY + lax.rem(y - b // NX + NY, NY)
            at = pl.ds(pl.multiple_of((half * HELD + b) * 128, 128), 128)
            turned = panels[place, 0:128, :]
            notes = panels[place, 128:144, :].astype(f32)
            left_all[:, at] = turned
            right[at, 128:256] = turned.astype(f32).T.astype(bf16)
            part = source[b]
            right[at, 0:128] = part
            wide = part.astype(f32)
            wide = wide * wide
            high = wide.astype(bf16)
            squares[at, 0:128] = high
            squares[at, 128:256] = (wide - high.astype(f32)).astype(bf16)
            hit = jnp.zeros((HELD, 128), f32)
            for k in range(8):
                hit = jnp.where(notes[k : k + 1, :] == ids, 1.0, hit)
            marks[:, at] = hit
            norms[...] += hit * (notes[8:9, :] + notes[9:10, :])

    chunk = 2048

    @pl.loop(0, 4)
    def _(g):
        @pl.loop(0, 4)
        def _(k):
            at = pl.ds(pl.multiple_of(k * chunk, chunk), chunk)
            hits = marks[pl.ds(pl.multiple_of(g * 8, 8), 8), at]
            for j in range(8):
                row = jnp.broadcast_to(hits[j : j + 1, :], (16, chunk)).astype(bf16)
                for r in range(8):
                    left[j * 128 + r * 16 : j * 128 + r * 16 + 16, :] = (
                        left_all[r * 16 : r * 16 + 16, at] * row
                    )
            product = jnp.dot(left[...], right[at, :], preferred_element_type=f32)

            @pl.when(k == 0)
            def _():
                total[...] = product

            @pl.when(k > 0)
            def _():
                total[...] += product

        for j in range(8):
            out[g * 8 + j, 0:128, :] = total[j * 128 : (j + 1) * 128, 0:128]
            quarter = pl.ds(pl.multiple_of(j * 128 + 32 * x, 32), 32)
            out[g * 8 + j, 128:160, :] = total[quarter, 128:256]

    sums = jnp.dot(marks[...].astype(bf16), squares[...], preferred_element_type=f32)
    sums = sums[:, 0:128] + sums[:, 128:256]
    scale = jnp.broadcast_to(jnp.sum(norms[...], axis=1, keepdims=True), (HELD, 128))
    for e in range(HELD):
        out[e, 160:168, :] = jnp.concatenate(
            [sums[e : e + 1], scale[e : e + 1], jnp.zeros((6, 128), f32)], axis=0
        )


def gram(where, wanted, own, other, panels):
    return pl.pallas_call(
        gram_kernel,
        out_shape=jax.ShapeDtypeStruct((HELD, ROWS, 128), f32),
        in_specs=[SMEM] + [VMEM] * 4,
        out_specs=VMEM,
        scratch_shapes=[
            pltpu.VMEM((128, 8192), bf16),
            pltpu.VMEM((8192, 256), bf16),
            pltpu.VMEM((8192, 256), bf16),
            pltpu.VMEM((HELD, 8192), f32),
            pltpu.VMEM((1024, 2048), bf16),
            pltpu.VMEM((1024, 256), f32),
            pltpu.VMEM((HELD, 128), f32),
        ],
        compiler_params=pltpu.CompilerParams(vmem_limit_bytes=48 * 1024 * 1024),
        cost_estimate=pl.CostEstimate(
            flops=2 * 4096 * 8192 * 256, bytes_accessed=8 << 20, transcendentals=0
        ),
    )(where, wanted, own, other, panels)


def parts_of(value, count):
    found = []
    for _ in range(count):
        part = value.astype(bf16)
        found.append(part)
        value = value - part.astype(f32)
    return found


def refit_kernel(where, s0, s1, s2, s3, shared, held, out, normed, scaled, inverse):
    x, y = where[0], where[2]
    scaling = s0[161:162, :] + EPSILON
    a = lax.broadcasted_iota(jnp.int32, (128, 128), 0)
    b = lax.broadcasted_iota(jnp.int32, (128, 128), 1)
    for step, sums in enumerate((s0, s1, s2, s3)):
        q = lax.rem(x - step + NX, NX)
        diagonal = sums[160:161, :] / scaling + DAMPING
        high, low = parts_of(sums[0:128, :] / scaling / diagonal, 2)
        at = pl.ds(pl.multiple_of(q * 128, 128), 128)
        scaled[0:128, at] = high
        scaled[128:256, at] = low
        scaled[256:384, at] = high
        rows = lax.broadcasted_iota(jnp.int32, (32, 128), 0) + q * 32
        lanes = lax.broadcasted_iota(jnp.int32, (32, 128), 1)
        damped = sums[128:160, :] / scaling + jnp.where(rows == lanes, DAMPING, 0.0)
        for k, part in enumerate(parts_of(damped, 3)):
            normed[pl.ds(pl.multiple_of(k * 128 + q * 32, 32), 32), :] = part
    for q in range(NY):
        part = [shared[q, 240 + 16 * k : 256 + 16 * k, :] for k in range(3)]
        for k, source in enumerate((0, 1, 0, 2, 1, 0)):
            inverse[k * 128 + q * 16 : k * 128 + q * 16 + 16, :] = part[source]

    @pl.loop(0, NY)
    def _(q):
        numbers = shared[q, 192:240, :]
        spread = []
        for part in range(4):
            pick = jnp.where(a == part * 32 + b // 4, 1.0, 0.0).astype(bf16)
            spread.append(jnp.dot(numbers, pick, preferred_element_type=f32))
        number = jnp.concatenate(spread, axis=0)
        lane = lax.broadcasted_iota(jnp.int32, (192, 128), 1) % 4
        code = number.astype(jnp.int32)
        kept = jnp.where(lane == 0, 0b000111, jnp.where(lane == 1, 0b011001, jnp.where(lane == 2, 0b101010, 0b110100)))
        mask = ((kept >> code) & 1).astype(f32)
        panel = shared[q, 0:192, :].astype(f32)
        dropped = ((1.0 - mask) * panel).astype(bf16)
        step = jnp.dot(jnp.concatenate([dropped] * 3, axis=1), normed[...], preferred_element_type=f32)
        high, middle, low = parts_of(step, 3)
        step = jnp.dot(
            jnp.concatenate([high, high, middle, high, middle, low], axis=1),
            inverse[...],
            preferred_element_type=f32,
        )
        refitted = mask * (panel + step)
        high, low = parts_of(refitted - panel, 2)
        correction = jnp.dot(
            jnp.concatenate([high, high, low], axis=1), scaled[...], preferred_element_type=f32
        )
        for k in range(4):
            for half in range(2):
                piece = held[16 * k + 2 * q + half, :, :].astype(f32)
                fixed = piece - correction[half * 96 : (half + 1) * 96, k * 128 : (k + 1) * 128]
                out[pl.ds(pl.multiple_of(q * 192 + half * 96, 32), 96), k * 128 : (k + 1) * 128] = fixed.astype(bf16)

        @pl.when(y == 0)
        def _():
            out[pl.ds(pl.multiple_of(q * 192, 64), 192), 0:128] = refitted.astype(bf16)


def refit(where, sums, shared, held):
    return pl.pallas_call(
        refit_kernel,
        out_shape=jax.ShapeDtypeStruct((FF, 512), bf16),
        in_specs=[SMEM] + [VMEM] * 6,
        out_specs=VMEM,
        scratch_shapes=[
            pltpu.VMEM((384, 128), bf16),
            pltpu.VMEM((384, 512), bf16),
            pltpu.VMEM((768, 128), bf16),
        ],
        compiler_params=pltpu.CompilerParams(vmem_limit_bytes=32 * 1024 * 1024),
    )(where, *sums, shared, held)


def swap(value, axis, size, step):
    return lax.ppermute(value, axis, [(i, (i + step) % size) for i in range(size)])


def after(value, *others):
    return lax.optimization_barrier((value, *others))[0]


def shards(tokens, routes, old_slots, new_slots, weights, patterns, inverse):
    x, y, z, c = (lax.axis_index(name) for name in ("x", "y", "z", "c"))
    me = (x * NZ + z) * NC + c
    where = jnp.stack([x, c, y]).astype(jnp.int32)
    slot = jnp.arange(64, dtype=jnp.int32)
    source = jnp.sum(jnp.where(old_slots[None, :] == new_slots[:, None], slot[None, :], 0), axis=1)
    order = new_slots.reshape(NX, NZ, NC).transpose(2, 1, 0).reshape(NC, HELD)
    wanted = jnp.broadcast_to(
        lax.dynamic_index_in_dim(order, c, 0, keepdims=False)[:, None], (HELD, 128)
    ).astype(f32)

    blocks, notes = prepare(tokens, routes, weights[0, :, 0:PANEL])
    own = lax.all_to_all(blocks, ("y", "x"), 0, 0, tiled=True)

    def note(step):
        return lax.dynamic_index_in_dim(notes, (y + step) % NY, 0, keepdims=False)

    came = [note(0)] + [swap(note(step), "y", NY, step) for step in range(1, NY)]
    own, *came = lax.optimization_barrier((own, *came))
    panels, rows = sort(where, came)
    panels = lax.all_gather(panels, ("x", "c"), axis=0, tiled=False).reshape(64, 144, 128)
    pieces = pack(
        weights[0],
        lax.dynamic_slice_in_dim(patterns[0], y * 192, 192, 0),
        lax.dynamic_slice_in_dim(inverse[0], y * 16, 16, 0),
        rows,
    )
    spread = lax.all_to_all(pieces, EXPERT, 0, 0, tiled=True)
    other = swap(own, "c", NC, 1)
    tails = jnp.take(spread[:, 96:104], source, axis=0, mode="clip")
    tails = lax.all_to_all(tails, EXPERT, 0, 0, tiled=True)
    shared = jnp.concatenate(
        [tails[:, 2:5].reshape(192, 128), tails[:, 0:2].reshape(128, 128)[0:96]], axis=0
    )
    shared = lax.all_gather(shared, "y", axis=0, tiled=False)
    held = jnp.take(spread[:, 0:96], source, axis=0, mode="clip")
    held = lax.all_to_all(after(held, tails), EXPERT, 0, 0, tiled=True)

    sums = gram(where, wanted, own, other, panels)
    sums = lax.psum_scatter(sums, "z", scatter_dimension=0, tiled=True)
    sums = after(sums, shared)

    def column(step):
        return lax.dynamic_index_in_dim(sums, (x + step) % NX, 0, keepdims=False)

    sums = [column(0)] + [swap(column(step), "x", NX, step) for step in range(1, NX)]
    return refit(where, sums, shared, held)[None]


def solution(mesh):
    grid = Mesh(mesh.devices.reshape(NY, NX, NZ, NC), ("y", "x", "z", "c"))
    placed = (
        P(("y", "x", "z", "c"), None),
        P(("y", "x", "z", "c"), None),
        P(),
        P(),
        P(EXPERT, None, "y"),
        P(EXPERT, None, None),
        P(EXPERT, None, None),
    )
    return jax.shard_map(
        shards, mesh=grid, in_specs=placed, out_specs=P(EXPERT, None, "y"), check_vma=False
    )
```

```python
import jax
import jax.numpy as jnp
from jax import lax
from jax.experimental import pallas as pl
from jax.experimental.pallas import tpu as pltpu
from jax.sharding import Mesh
from jax.sharding import PartitionSpec as P

D = 4096
FF = 1536
PANEL = 128
EPSILON = 1e-06
DAMPING = 0.01
NY, NX, NZ, NC = 8, 4, 8, 2
HELD = 32
ROWS = 168
EXPERT = ("x", "z", "c")
bf16 = jnp.bfloat16
f32 = jnp.float32
VMEM = pl.BlockSpec(memory_space=pltpu.VMEM)
SMEM = pl.BlockSpec(memory_space=pltpu.SMEM)


def pack_kernel(weights, patterns, inverse, pieces):
    numbers = patterns[...].astype(f32)
    rest = inverse[...]
    parts = []
    for q in range(3):
        piece = rest.astype(bf16).astype(f32)
        parts.append(piece)
        rest = rest - piece
    extra = jnp.concatenate(
        [numbers[48 * q : 48 * (q + 1)] for q in range(4)], axis=1
    )
    extra = jnp.concatenate([extra] + parts + [jnp.zeros((32, 128), f32)], axis=0)
    for p in range(64):
        k, q = p // 16, p % 16
        pieces[p, 0:96, :] = weights[96 * q : 96 * (q + 1), 128 * k : 128 * (k + 1)]
        pieces[p, 96:104, :] = jnp.concatenate(
            [extra[2 * p : 2 * p + 2], jnp.zeros((6, 128), f32)], axis=0
        ).astype(bf16)


def pack(weights, patterns, inverse):
    return pl.pallas_call(
        pack_kernel,
        out_shape=jax.ShapeDtypeStruct((64, 104, 128), bf16),
        in_specs=[VMEM] * 3,
        out_specs=VMEM,
        compiler_params=pltpu.CompilerParams(vmem_limit_bytes=16 * 1024 * 1024),
    )(weights, patterns, inverse)


def join_kernel(*refs):
    for s in range(NY):
        refs[NY][s * 144 : (s + 1) * 144, :] = refs[s][...]


def join(came):
    return pl.pallas_call(
        join_kernel,
        out_shape=jax.ShapeDtypeStruct((NY * 144, 128), bf16),
        in_specs=[VMEM] * NY,
        out_specs=VMEM,
        compiler_params=pltpu.CompilerParams(vmem_limit_bytes=16 * 1024 * 1024),
    )(*came)


def prep_kernel(tokens, routes, blocks, panel):
    squares = jnp.zeros((128, 128), f32)
    for s in range(32):
        part = tokens[:, s * 128 : (s + 1) * 128]
        blocks[s] = part
        wide = part.astype(f32)
        squares = squares + wide * wide
    panel[0:128, :] = tokens[:, 0:128].astype(f32).T.astype(bf16)
    norms = jnp.sum(squares.T, axis=0, keepdims=True) * (1.0 / D)
    high = norms.astype(bf16).astype(f32)
    named = jnp.concatenate(
        [routes[...].astype(f32), jnp.zeros((128, 120), f32)], axis=1
    ).T
    panel[128:144, :] = jnp.concatenate(
        [named[0:8], high, norms - high, jnp.zeros((6, 128), f32)], axis=0
    ).astype(bf16)


def prepare(tokens, routes):
    return pl.pallas_call(
        prep_kernel,
        out_shape=(
            jax.ShapeDtypeStruct((32, 128, 128), bf16),
            jax.ShapeDtypeStruct((144, 128), bf16),
        ),
        in_specs=[VMEM] * 2,
        out_specs=(VMEM,) * 2,
        compiler_params=pltpu.CompilerParams(vmem_limit_bytes=16 * 1024 * 1024),
    )(tokens, routes)


def gram_kernel(where, wanted, own, other, panels, out, left_all, right, squares, marks, left, total, norms):
    x, c, y = where[0], where[1], where[2]
    ids = wanted[...]
    norms[...] = jnp.zeros_like(norms)
    for half, source in ((0, own), (1, other)):
        core = c if half == 0 else 1 - c

        @pl.loop(0, HELD)
        def _(b):
            place = ((b % NX) * NC + core) * NY + lax.rem(y - b // NX + NY, NY)
            at = pl.ds(pl.multiple_of((half * HELD + b) * 128, 128), 128)
            turned = panels[place, 0:128, :]
            notes = panels[place, 128:144, :].astype(f32)
            left_all[:, at] = turned
            right[at, 128:256] = turned.astype(f32).T.astype(bf16)
            part = source[b]
            right[at, 0:128] = part
            wide = part.astype(f32)
            wide = wide * wide
            high = wide.astype(bf16)
            squares[at, 0:128] = high
            squares[at, 128:256] = (wide - high.astype(f32)).astype(bf16)
            hit = jnp.zeros((HELD, 128), f32)
            for k in range(8):
                hit = jnp.where(notes[k : k + 1, :] == ids, 1.0, hit)
            marks[:, at] = hit
            norms[...] += hit * (notes[8:9, :] + notes[9:10, :])

    chunk = 2048

    @pl.loop(0, 4)
    def _(g):
        @pl.loop(0, 4)
        def _(k):
            at = pl.ds(pl.multiple_of(k * chunk, chunk), chunk)
            hits = marks[pl.ds(pl.multiple_of(g * 8, 8), 8), at]
            for j in range(8):
                row = jnp.broadcast_to(hits[j : j + 1, :], (16, chunk)).astype(bf16)
                for r in range(8):
                    left[j * 128 + r * 16 : j * 128 + r * 16 + 16, :] = (
                        left_all[r * 16 : r * 16 + 16, at] * row
                    )
            product = jnp.dot(left[...], right[at, :], preferred_element_type=f32)

            @pl.when(k == 0)
            def _():
                total[...] = product

            @pl.when(k > 0)
            def _():
                total[...] += product

        for j in range(8):
            out[g * 8 + j, 0:128, :] = total[j * 128 : (j + 1) * 128, 0:128]
            quarter = pl.ds(pl.multiple_of(j * 128 + 32 * x, 32), 32)
            out[g * 8 + j, 128:160, :] = total[quarter, 128:256]

    sums = jnp.dot(marks[...].astype(bf16), squares[...], preferred_element_type=f32)
    sums = sums[:, 0:128] + sums[:, 128:256]
    scale = jnp.broadcast_to(jnp.sum(norms[...], axis=1, keepdims=True), (HELD, 128))
    for e in range(HELD):
        out[e, 160:168, :] = jnp.concatenate(
            [sums[e : e + 1], scale[e : e + 1], jnp.zeros((6, 128), f32)], axis=0
        )


def gram(where, wanted, own, other, panels):
    return pl.pallas_call(
        gram_kernel,
        out_shape=jax.ShapeDtypeStruct((HELD, ROWS, 128), f32),
        in_specs=[SMEM] + [VMEM] * 4,
        out_specs=VMEM,
        scratch_shapes=[
            pltpu.VMEM((128, 8192), bf16),
            pltpu.VMEM((8192, 256), bf16),
            pltpu.VMEM((8192, 256), bf16),
            pltpu.VMEM((HELD, 8192), f32),
            pltpu.VMEM((1024, 2048), bf16),
            pltpu.VMEM((1024, 256), f32),
            pltpu.VMEM((HELD, 128), f32),
        ],
        compiler_params=pltpu.CompilerParams(vmem_limit_bytes=48 * 1024 * 1024),
        cost_estimate=pl.CostEstimate(
            flops=2 * 4096 * 8192 * 256, bytes_accessed=8 << 20, transcendentals=0
        ),
    )(where, wanted, own, other, panels)


def parts_of(value, count):
    found = []
    for _ in range(count):
        part = value.astype(bf16)
        found.append(part)
        value = value - part.astype(f32)
    return found


def refit_kernel(where, total, shared, held, out, normed, scaled, inverse):
    y = where[2]
    scaling = total[0, 161:162, :] + EPSILON
    a = lax.broadcasted_iota(jnp.int32, (128, 128), 0)
    b = lax.broadcasted_iota(jnp.int32, (128, 128), 1)
    for q in range(NX):
        sums = total[q]
        diagonal = sums[160:161, :] / scaling + DAMPING
        high, low = parts_of(sums[0:128, :] / scaling / diagonal, 2)
        at = slice(q * 128, (q + 1) * 128)
        scaled[0:128, at] = high
        scaled[128:256, at] = low
        scaled[256:384, at] = high
        rows = lax.broadcasted_iota(jnp.int32, (32, 128), 0) + q * 32
        lanes = lax.broadcasted_iota(jnp.int32, (32, 128), 1)
        damped = sums[128:160, :] / scaling + jnp.where(rows == lanes, DAMPING, 0.0)
        for k, part in enumerate(parts_of(damped, 3)):
            normed[k * 128 + q * 32 : k * 128 + q * 32 + 32, :] = part
    for q in range(NY):
        part = [shared[q, 240 + 16 * k : 256 + 16 * k, :] for k in range(3)]
        for k, source in enumerate((0, 1, 0, 2, 1, 0)):
            inverse[k * 128 + q * 16 : k * 128 + q * 16 + 16, :] = part[source]

    @pl.loop(0, NY)
    def _(q):
        numbers = shared[q, 192:240, :]
        spread = []
        for part in range(4):
            pick = jnp.where(a == part * 32 + b // 4, 1.0, 0.0).astype(bf16)
            spread.append(jnp.dot(numbers, pick, preferred_element_type=f32))
        number = jnp.concatenate(spread, axis=0)
        lane = lax.broadcasted_iota(jnp.int32, (192, 128), 1) % 4
        code = number.astype(jnp.int32)
        kept = jnp.where(lane == 0, 0b000111, jnp.where(lane == 1, 0b011001, jnp.where(lane == 2, 0b101010, 0b110100)))
        mask = ((kept >> code) & 1).astype(f32)
        panel = shared[q, 0:192, :].astype(f32)
        dropped = ((1.0 - mask) * panel).astype(bf16)
        step = jnp.dot(jnp.concatenate([dropped] * 3, axis=1), normed[...], preferred_element_type=f32)
        high, middle, low = parts_of(step, 3)
        step = jnp.dot(
            jnp.concatenate([high, high, middle, high, middle, low], axis=1),
            inverse[...],
            preferred_element_type=f32,
        )
        refitted = mask * (panel + step)
        high, low = parts_of(refitted - panel, 2)
        correction = jnp.dot(
            jnp.concatenate([high, high, low], axis=1), scaled[...], preferred_element_type=f32
        )
        for k in range(4):
            for half in range(2):
                piece = held[16 * k + 2 * q + half, 0:96, :].astype(f32)
                fixed = piece - correction[half * 96 : (half + 1) * 96, k * 128 : (k + 1) * 128]
                out[pl.ds(pl.multiple_of(q * 192 + half * 96, 32), 96), k * 128 : (k + 1) * 128] = fixed.astype(bf16)

        @pl.when(y == 0)
        def _():
            out[pl.ds(pl.multiple_of(q * 192, 64), 192), 0:128] = refitted.astype(bf16)


def refit(where, sums, shared, held):
    return pl.pallas_call(
        refit_kernel,
        out_shape=jax.ShapeDtypeStruct((FF, 512), bf16),
        in_specs=[SMEM] + [VMEM] * 3,
        out_specs=VMEM,
        scratch_shapes=[
            pltpu.VMEM((384, 128), bf16),
            pltpu.VMEM((384, 512), bf16),
            pltpu.VMEM((768, 128), bf16),
        ],
        compiler_params=pltpu.CompilerParams(vmem_limit_bytes=32 * 1024 * 1024),
    )(where, sums, shared, held)


def swap(value, axis, size, step):
    return lax.ppermute(value, axis, [(i, (i + step) % size) for i in range(size)])


def after(value, *others):
    return lax.optimization_barrier((value, *others))[0]


def shards(tokens, routes, old_slots, new_slots, weights, patterns, inverse):
    x, y, z, c = (lax.axis_index(name) for name in ("x", "y", "z", "c"))
    me = (x * NZ + z) * NC + c
    where = jnp.stack([x, c, y]).astype(jnp.int32)
    slot = jnp.arange(64, dtype=jnp.int32)
    source = jnp.sum(jnp.where(old_slots[None, :] == new_slots[:, None], slot[None, :], 0), axis=1)
    order = new_slots.reshape(NX, NZ, NC).transpose(2, 1, 0).reshape(NC, HELD)
    wanted = jnp.broadcast_to(
        lax.dynamic_index_in_dim(order, c, 0, keepdims=False)[:, None], (HELD, 128)
    ).astype(f32)

    pieces = pack(
        weights[0],
        lax.dynamic_slice_in_dim(patterns[0], y * 192, 192, 0),
        lax.dynamic_slice_in_dim(inverse[0], y * 16, 16, 0),
    )
    spread = lax.all_to_all(pieces, EXPERT, 0, 0, tiled=True)
    blocks, panel = prepare(tokens, routes)
    came = [panel] + [swap(panel, "y", NY, step) for step in range(1, NY)]
    spread, *came = lax.optimization_barrier((spread, *came))
    panels = lax.all_gather(join(came), ("x", "c"), axis=0, tiled=False).reshape(64, 144, 128)
    own = lax.all_to_all(after(blocks, spread), ("y", "x"), 0, 0, tiled=True)
    other = swap(own, "c", NC, 1)
    spread = jnp.take(spread, source, axis=0, mode="clip")
    held = lax.all_to_all(after(spread, own), EXPERT, 0, 0, tiled=True)

    sums = gram(where, wanted, own, other, panels)
    sums = lax.psum_scatter(after(sums, held), "z", scatter_dimension=0, tiled=True)
    moved = held[0:16, 0:96].reshape(NY, 192, 128)
    moved = lax.all_to_all(moved, "y", 0, 0, tiled=True)[0]
    shared = jnp.concatenate([moved, held[:, 96:98].reshape(128, 128)[0:96]], axis=0)
    shared = lax.all_gather(shared, "y", axis=0, tiled=False)
    sums = lax.all_to_all(after(sums, shared), "x", 0, 0, tiled=True)
    return refit(where, sums, shared, held)[None]


def solution(mesh):
    grid = Mesh(mesh.devices.reshape(NY, NX, NZ, NC), ("y", "x", "z", "c"))
    placed = (
        P(("y", "x", "z", "c"), None),
        P(("y", "x", "z", "c"), None),
        P(),
        P(),
        P(EXPERT, None, "y"),
        P(EXPERT, None, None),
        P(EXPERT, None, None),
    )
    return jax.shard_map(
        shards, mesh=grid, in_specs=placed, out_specs=P(EXPERT, None, "y"), check_vma=False
    )
```

```python
import jax
import jax.numpy as jnp
from jax import lax
from jax.experimental import pallas as pl
from jax.experimental.pallas import tpu as pltpu
from jax.sharding import Mesh
from jax.sharding import PartitionSpec as P

D = 4096
FF = 1536
PANEL = 128
EPSILON = 1e-06
DAMPING = 0.01
NY, NX, NZ, NC = 8, 4, 8, 2
HELD = 32
ROWS = 168
EXPERT = ("x", "z", "c")
bf16 = jnp.bfloat16
f32 = jnp.float32
VMEM = pl.BlockSpec(memory_space=pltpu.VMEM)
SMEM = pl.BlockSpec(memory_space=pltpu.SMEM)


def pack_kernel(weights, patterns, inverse, pieces):
    numbers = patterns[...].astype(f32)
    rest = inverse[...]
    parts = []
    for q in range(3):
        piece = rest.astype(bf16).astype(f32)
        parts.append(piece)
        rest = rest - piece
    extra = jnp.concatenate(
        [numbers[48 * q : 48 * (q + 1)] for q in range(4)], axis=1
    )
    extra = jnp.concatenate([extra] + parts + [jnp.zeros((32, 128), f32)], axis=0)
    for p in range(64):
        k, q = p // 16, p % 16
        pieces[p, 0:96, :] = weights[96 * q : 96 * (q + 1), 128 * k : 128 * (k + 1)]
        pieces[p, 96:104, :] = jnp.concatenate(
            [extra[2 * p : 2 * p + 2], jnp.zeros((6, 128), f32)], axis=0
        ).astype(bf16)


def pack(weights, patterns, inverse):
    return pl.pallas_call(
        pack_kernel,
        out_shape=jax.ShapeDtypeStruct((64, 104, 128), bf16),
        in_specs=[VMEM] * 3,
        out_specs=VMEM,
        compiler_params=pltpu.CompilerParams(vmem_limit_bytes=16 * 1024 * 1024),
    )(weights, patterns, inverse)


def sort_kernel(where, *refs):
    came, panels, slices = refs[:NY], refs[NY], refs[NY + 1 :]
    for s in range(NY):
        panels[s * 144 : (s + 1) * 144, :] = came[s][512:656, :]
        for step in range(NX):
            at = pl.multiple_of(lax.rem(where[0] + step, NX) * 128, 128)
            slices[step][s] = came[s][pl.ds(at, 128), :]


def sort(where, came):
    return pl.pallas_call(
        sort_kernel,
        out_shape=(jax.ShapeDtypeStruct((NY * 144, 128), bf16),)
        + (jax.ShapeDtypeStruct((NY, 128, 128), bf16),) * NX,
        in_specs=[SMEM] + [VMEM] * NY,
        out_specs=(VMEM,) * (1 + NX),
        compiler_params=pltpu.CompilerParams(vmem_limit_bytes=16 * 1024 * 1024),
    )(where, *came)


def prep_kernel(tokens, routes, blocks):
    squares = jnp.zeros((128, 128), f32)
    for s in range(32):
        part = tokens[:, s * 128 : (s + 1) * 128]
        blocks[s // NX, (s % NX) * 128 : (s % NX) * 128 + 128, :] = part
        wide = part.astype(f32)
        squares = squares + wide * wide
    turned = tokens[:, 0:128].astype(f32).T.astype(bf16)
    norms = jnp.sum(squares.T, axis=0, keepdims=True) * (1.0 / D)
    high = norms.astype(bf16).astype(f32)
    named = jnp.concatenate(
        [routes[...].astype(f32), jnp.zeros((128, 120), f32)], axis=1
    ).T
    notes = jnp.concatenate(
        [named[0:8], high, norms - high, jnp.zeros((6, 128), f32)], axis=0
    ).astype(bf16)
    for s in range(NY):
        blocks[s, 512:640, :] = turned
        blocks[s, 640:656, :] = notes


def prepare(tokens, routes):
    return pl.pallas_call(
        prep_kernel,
        out_shape=jax.ShapeDtypeStruct((NY, 656, 128), bf16),
        in_specs=[VMEM] * 2,
        out_specs=VMEM,
        compiler_params=pltpu.CompilerParams(vmem_limit_bytes=16 * 1024 * 1024),
    )(tokens, routes)


def gram_kernel(where, wanted, *refs):
    parts, panels, out = refs[: 2 * NX], refs[2 * NX], refs[2 * NX + 1]
    left_all, right, squares, marks, left, total, norms = refs[2 * NX + 2 :]
    x, c = where[0], where[1]
    ids = wanted[...]
    norms[...] = jnp.zeros_like(norms)
    for number, source in enumerate(parts):
        core = c if number < NX else 1 - c
        first = (lax.rem(x - number % NX + NX, NX) * NC + core) * NY

        @pl.loop(0, NY)
        def _(b, number=number, source=source, first=first):
            place = first + b
            at = pl.ds(pl.multiple_of((number * NY + b) * 128, 128), 128)
            turned = panels[place, 0:128, :]
            notes = panels[place, 128:144, :].astype(f32)
            left_all[:, at] = turned
            right[at, 128:256] = turned.astype(f32).T.astype(bf16)
            part = source[b]
            right[at, 0:128] = part
            wide = part.astype(f32)
            wide = wide * wide
            high = wide.astype(bf16)
            squares[at, 0:128] = high
            squares[at, 128:256] = (wide - high.astype(f32)).astype(bf16)
            hit = jnp.zeros((HELD, 128), f32)
            for k in range(8):
                hit = jnp.where(notes[k : k + 1, :] == ids, 1.0, hit)
            marks[:, at] = hit
            norms[...] += hit * (notes[8:9, :] + notes[9:10, :])

    chunk = 2048

    @pl.loop(0, 4)
    def _(g):
        @pl.loop(0, 4)
        def _(k):
            at = pl.ds(pl.multiple_of(k * chunk, chunk), chunk)
            hits = marks[pl.ds(pl.multiple_of(g * 8, 8), 8), at]
            for j in range(8):
                row = jnp.broadcast_to(hits[j : j + 1, :], (16, chunk)).astype(bf16)
                for r in range(8):
                    left[j * 128 + r * 16 : j * 128 + r * 16 + 16, :] = (
                        left_all[r * 16 : r * 16 + 16, at] * row
                    )
            product = jnp.dot(left[...], right[at, :], preferred_element_type=f32)

            @pl.when(k == 0)
            def _():
                total[...] = product

            @pl.when(k > 0)
            def _():
                total[...] += product

        for j in range(8):
            out[g * 8 + j, 0:128, :] = total[j * 128 : (j + 1) * 128, 0:128]
            quarter = pl.ds(pl.multiple_of(j * 128 + 32 * x, 32), 32)
            out[g * 8 + j, 128:160, :] = total[quarter, 128:256]

    sums = jnp.dot(marks[...].astype(bf16), squares[...], preferred_element_type=f32)
    sums = sums[:, 0:128] + sums[:, 128:256]
    scale = jnp.broadcast_to(jnp.sum(norms[...], axis=1, keepdims=True), (HELD, 128))
    for e in range(HELD):
        out[e, 160:168, :] = jnp.concatenate(
            [sums[e : e + 1], scale[e : e + 1], jnp.zeros((6, 128), f32)], axis=0
        )


def gram(where, wanted, parts, panels):
    return pl.pallas_call(
        gram_kernel,
        out_shape=jax.ShapeDtypeStruct((HELD, ROWS, 128), f32),
        in_specs=[SMEM] + [VMEM] * (2 + 2 * NX),
        out_specs=VMEM,
        scratch_shapes=[
            pltpu.VMEM((128, 8192), bf16),
            pltpu.VMEM((8192, 256), bf16),
            pltpu.VMEM((8192, 256), bf16),
            pltpu.VMEM((HELD, 8192), f32),
            pltpu.VMEM((1024, 2048), bf16),
            pltpu.VMEM((1024, 256), f32),
            pltpu.VMEM((HELD, 128), f32),
        ],
        compiler_params=pltpu.CompilerParams(vmem_limit_bytes=48 * 1024 * 1024),
        cost_estimate=pl.CostEstimate(
            flops=2 * 4096 * 8192 * 256, bytes_accessed=8 << 20, transcendentals=0
        ),
    )(where, wanted, *parts, panels)


def parts_of(value, count):
    found = []
    for _ in range(count):
        part = value.astype(bf16)
        found.append(part)
        value = value - part.astype(f32)
    return found


def refit_kernel(where, total, shared, held, out, normed, scaled, inverse):
    y = where[2]
    scaling = total[0, 161:162, :] + EPSILON
    a = lax.broadcasted_iota(jnp.int32, (128, 128), 0)
    b = lax.broadcasted_iota(jnp.int32, (128, 128), 1)
    for q in range(NX):
        sums = total[q]
        diagonal = sums[160:161, :] / scaling + DAMPING
        high, low = parts_of(sums[0:128, :] / scaling / diagonal, 2)
        at = slice(q * 128, (q + 1) * 128)
        scaled[0:128, at] = high
        scaled[128:256, at] = low
        scaled[256:384, at] = high
        rows = lax.broadcasted_iota(jnp.int32, (32, 128), 0) + q * 32
        lanes = lax.broadcasted_iota(jnp.int32, (32, 128), 1)
        damped = sums[128:160, :] / scaling + jnp.where(rows == lanes, DAMPING, 0.0)
        for k, part in enumerate(parts_of(damped, 3)):
            normed[k * 128 + q * 32 : k * 128 + q * 32 + 32, :] = part
    for q in range(NY):
        part = [shared[q, 240 + 16 * k : 256 + 16 * k, :] for k in range(3)]
        for k, source in enumerate((0, 1, 0, 2, 1, 0)):
            inverse[k * 128 + q * 16 : k * 128 + q * 16 + 16, :] = part[source]

    @pl.loop(0, NY)
    def _(q):
        numbers = shared[q, 192:240, :]
        spread = []
        for part in range(4):
            pick = jnp.where(a == part * 32 + b // 4, 1.0, 0.0).astype(bf16)
            spread.append(jnp.dot(numbers, pick, preferred_element_type=f32))
        number = jnp.concatenate(spread, axis=0)
        lane = lax.broadcasted_iota(jnp.int32, (192, 128), 1) % 4
        code = number.astype(jnp.int32)
        kept = jnp.where(lane == 0, 0b000111, jnp.where(lane == 1, 0b011001, jnp.where(lane == 2, 0b101010, 0b110100)))
        mask = ((kept >> code) & 1).astype(f32)
        panel = shared[q, 0:192, :].astype(f32)
        dropped = ((1.0 - mask) * panel).astype(bf16)
        step = jnp.dot(jnp.concatenate([dropped] * 3, axis=1), normed[...], preferred_element_type=f32)
        high, middle, low = parts_of(step, 3)
        step = jnp.dot(
            jnp.concatenate([high, high, middle, high, middle, low], axis=1),
            inverse[...],
            preferred_element_type=f32,
        )
        refitted = mask * (panel + step)
        high, low = parts_of(refitted - panel, 2)
        correction = jnp.dot(
            jnp.concatenate([high, high, low], axis=1), scaled[...], preferred_element_type=f32
        )
        for k in range(4):
            for half in range(2):
                piece = held[16 * k + 2 * q + half, 0:96, :].astype(f32)
                fixed = piece - correction[half * 96 : (half + 1) * 96, k * 128 : (k + 1) * 128]
                out[pl.ds(pl.multiple_of(q * 192 + half * 96, 32), 96), k * 128 : (k + 1) * 128] = fixed.astype(bf16)

        @pl.when(y == 0)
        def _():
            out[pl.ds(pl.multiple_of(q * 192, 64), 192), 0:128] = refitted.astype(bf16)


def refit(where, sums, shared, held):
    return pl.pallas_call(
        refit_kernel,
        out_shape=jax.ShapeDtypeStruct((FF, 512), bf16),
        in_specs=[SMEM] + [VMEM] * 3,
        out_specs=VMEM,
        scratch_shapes=[
            pltpu.VMEM((384, 128), bf16),
            pltpu.VMEM((384, 512), bf16),
            pltpu.VMEM((768, 128), bf16),
        ],
        compiler_params=pltpu.CompilerParams(vmem_limit_bytes=32 * 1024 * 1024),
    )(where, sums, shared, held)


def swap(value, axis, size, step):
    return lax.ppermute(value, axis, [(i, (i + step) % size) for i in range(size)])


def after(value, *others):
    return lax.optimization_barrier((value, *others))[0]


def shards(tokens, routes, old_slots, new_slots, weights, patterns, inverse):
    x, y, z, c = (lax.axis_index(name) for name in ("x", "y", "z", "c"))
    me = (x * NZ + z) * NC + c
    where = jnp.stack([x, c, y]).astype(jnp.int32)
    slot = jnp.arange(64, dtype=jnp.int32)
    source = jnp.sum(jnp.where(old_slots[None, :] == new_slots[:, None], slot[None, :], 0), axis=1)
    order = new_slots.reshape(NX, NZ, NC).transpose(2, 1, 0).reshape(NC, HELD)
    wanted = jnp.broadcast_to(
        lax.dynamic_index_in_dim(order, c, 0, keepdims=False)[:, None], (HELD, 128)
    ).astype(f32)

    pieces = pack(
        weights[0],
        lax.dynamic_slice_in_dim(patterns[0], y * 192, 192, 0),
        lax.dynamic_slice_in_dim(inverse[0], y * 16, 16, 0),
    )
    spread = lax.all_to_all(pieces, EXPERT, 0, 0, tiled=True)
    blocks = prepare(tokens, routes)

    def block(step):
        return lax.dynamic_index_in_dim(blocks, (y + step) % NY, 0, keepdims=False)

    came = [block(0)] + [swap(block(step), "y", NY, step) for step in range(1, NY)]
    spread, *came = lax.optimization_barrier((spread, *came))
    panels, *parts = sort(where, came)
    panels = lax.all_gather(panels, ("x", "c"), axis=0, tiled=False).reshape(64, 144, 128)
    spread = jnp.take(spread, source, axis=0, mode="clip")
    held = lax.all_to_all(spread, EXPERT, 0, 0, tiled=True)
    parts = parts[:1] + [swap(parts[step], "x", NX, step) for step in range(1, NX)]
    parts = parts + [swap(part, "c", NC, 1) for part in parts]

    sums = gram(where, wanted, parts, panels)
    sums = lax.psum_scatter(after(sums, held), "z", scatter_dimension=0, tiled=True)
    moved = held[0:16, 0:96].reshape(NY, 192, 128)
    moved = lax.all_to_all(moved, "y", 0, 0, tiled=True)[0]
    shared = jnp.concatenate([moved, held[:, 96:98].reshape(128, 128)[0:96]], axis=0)
    shared = lax.all_gather(shared, "y", axis=0, tiled=False)
    sums = lax.all_to_all(after(sums, shared), "x", 0, 0, tiled=True)
    return refit(where, sums, shared, held)[None]


def solution(mesh):
    grid = Mesh(mesh.devices.reshape(NY, NX, NZ, NC), ("y", "x", "z", "c"))
    placed = (
        P(("y", "x", "z", "c"), None),
        P(("y", "x", "z", "c"), None),
        P(),
        P(),
        P(EXPERT, None, "y"),
        P(EXPERT, None, None),
        P(EXPERT, None, None),
    )
    return jax.shard_map(
        shards, mesh=grid, in_specs=placed, out_specs=P(EXPERT, None, "y"), check_vma=False
    )
```

```python
import jax
import jax.numpy as jnp
from jax import lax
from jax.experimental import pallas as pl
from jax.experimental.pallas import tpu as pltpu
from jax.sharding import Mesh
from jax.sharding import PartitionSpec as P

D = 4096
FF = 1536
PANEL = 128
EPSILON = 1e-06
DAMPING = 0.01
NY, NX, NZ, NC = 8, 4, 8, 2
HELD = 32
ROWS = 168
EXPERT = ("x", "z", "c")
bf16 = jnp.bfloat16
f32 = jnp.float32
VMEM = pl.BlockSpec(memory_space=pltpu.VMEM)
SMEM = pl.BlockSpec(memory_space=pltpu.SMEM)


def pack_kernel(weights, patterns, inverse, pieces):
    numbers = patterns[...].astype(f32)
    rest = inverse[...]
    parts = []
    for q in range(3):
        piece = rest.astype(bf16).astype(f32)
        parts.append(piece)
        rest = rest - piece
    extra = jnp.concatenate(
        [numbers[48 * q : 48 * (q + 1)] for q in range(4)], axis=1
    )
    extra = jnp.concatenate([extra] + parts + [jnp.zeros((32, 128), f32)], axis=0)
    for p in range(64):
        k, q = p // 16, p % 16
        pieces[p, 0:96, :] = weights[96 * q : 96 * (q + 1), 128 * k : 128 * (k + 1)]
        pieces[p, 96:104, :] = jnp.concatenate(
            [extra[2 * p : 2 * p + 2], jnp.zeros((6, 128), f32)], axis=0
        ).astype(bf16)


def pack(weights, patterns, inverse):
    return pl.pallas_call(
        pack_kernel,
        out_shape=jax.ShapeDtypeStruct((64, 104, 128), bf16),
        in_specs=[VMEM] * 3,
        out_specs=VMEM,
        compiler_params=pltpu.CompilerParams(vmem_limit_bytes=16 * 1024 * 1024),
    )(weights, patterns, inverse)


def join_kernel(*refs):
    for s in range(NY):
        refs[NY][s * 144 : (s + 1) * 144, :] = refs[s][...]


def join(came):
    return pl.pallas_call(
        join_kernel,
        out_shape=jax.ShapeDtypeStruct((NY * 144, 128), bf16),
        in_specs=[VMEM] * NY,
        out_specs=VMEM,
        compiler_params=pltpu.CompilerParams(vmem_limit_bytes=16 * 1024 * 1024),
    )(*came)


def prep_kernel(tokens, routes, blocks, panel):
    squares = jnp.zeros((128, 128), f32)
    for s in range(32):
        part = tokens[:, s * 128 : (s + 1) * 128]
        blocks[s] = part
        wide = part.astype(f32)
        squares = squares + wide * wide
    panel[0:128, :] = tokens[:, 0:128].astype(f32).T.astype(bf16)
    norms = jnp.sum(squares.T, axis=0, keepdims=True) * (1.0 / D)
    high = norms.astype(bf16).astype(f32)
    named = jnp.concatenate(
        [routes[...].astype(f32), jnp.zeros((128, 120), f32)], axis=1
    ).T
    panel[128:144, :] = jnp.concatenate(
        [named[0:8], high, norms - high, jnp.zeros((6, 128), f32)], axis=0
    ).astype(bf16)


def prepare(tokens, routes):
    return pl.pallas_call(
        prep_kernel,
        out_shape=(
            jax.ShapeDtypeStruct((32, 128, 128), bf16),
            jax.ShapeDtypeStruct((144, 128), bf16),
        ),
        in_specs=[VMEM] * 2,
        out_specs=(VMEM,) * 2,
        compiler_params=pltpu.CompilerParams(vmem_limit_bytes=16 * 1024 * 1024),
    )(tokens, routes)


def gram_kernel(where, wanted, own, other, panels, out, left_all, right, squares, marks, left, total, norms):
    x, c, y = where[0], where[1], where[2]
    ids = wanted[...]
    norms[...] = jnp.zeros_like(norms)
    for half, source in ((0, own), (1, other)):
        core = c if half == 0 else 1 - c

        @pl.loop(0, HELD)
        def _(b):
            place = ((b % NX) * NC + core) * NY + lax.rem(y - b // NX + NY, NY)
            at = pl.ds(pl.multiple_of((half * HELD + b) * 128, 128), 128)
            turned = panels[place, 0:128, :]
            notes = panels[place, 128:144, :].astype(f32)
            left_all[:, at] = turned
            right[at, 128:256] = turned.astype(f32).T.astype(bf16)
            part = source[b]
            right[at, 0:128] = part
            wide = part.astype(f32)
            wide = wide * wide
            high = wide.astype(bf16)
            squares[at, 0:128] = high
            squares[at, 128:256] = (wide - high.astype(f32)).astype(bf16)
            hit = jnp.zeros((HELD, 128), f32)
            for k in range(8):
                hit = jnp.where(notes[k : k + 1, :] == ids, 1.0, hit)
            marks[:, at] = hit
            norms[...] += hit * (notes[8:9, :] + notes[9:10, :])

    chunk = 2048

    def build(g, k):
        at = slice(k * chunk, (k + 1) * chunk)
        hits = marks[pl.ds(pl.multiple_of(g * 8, 8), 8), at]
        for j in range(8):
            row = jnp.broadcast_to(hits[j : j + 1, :], (16, chunk)).astype(bf16)
            for r in range(8):
                left[k % 2, j * 128 + r * 16 : j * 128 + r * 16 + 16, :] = (
                    left_all[r * 16 : r * 16 + 16, at] * row
                )

    build(0, 0)

    @pl.loop(0, 4)
    def _(g):
        for k in range(4):
            product = jnp.dot(
                left[k % 2], right[k * chunk : (k + 1) * chunk, :], preferred_element_type=f32
            )
            build(g if k < 3 else lax.rem(g + 1, 4), (k + 1) % 4)
            if k == 0:
                total[...] = product
            else:
                total[...] += product

        for j in range(8):
            out[g * 8 + j, 0:128, :] = total[j * 128 : (j + 1) * 128, 0:128]
            quarter = pl.ds(pl.multiple_of(j * 128 + 32 * x, 32), 32)
            out[g * 8 + j, 128:160, :] = total[quarter, 128:256]

    sums = jnp.dot(marks[...].astype(bf16), squares[...], preferred_element_type=f32)
    sums = sums[:, 0:128] + sums[:, 128:256]
    scale = jnp.broadcast_to(jnp.sum(norms[...], axis=1, keepdims=True), (HELD, 128))
    for e in range(HELD):
        out[e, 160:168, :] = jnp.concatenate(
            [sums[e : e + 1], scale[e : e + 1], jnp.zeros((6, 128), f32)], axis=0
        )


def gram(where, wanted, own, other, panels):
    return pl.pallas_call(
        gram_kernel,
        out_shape=jax.ShapeDtypeStruct((HELD, ROWS, 128), f32),
        in_specs=[SMEM] + [VMEM] * 4,
        out_specs=VMEM,
        scratch_shapes=[
            pltpu.VMEM((128, 8192), bf16),
            pltpu.VMEM((8192, 256), bf16),
            pltpu.VMEM((8192, 256), bf16),
            pltpu.VMEM((HELD, 8192), f32),
            pltpu.VMEM((2, 1024, 2048), bf16),
            pltpu.VMEM((1024, 256), f32),
            pltpu.VMEM((HELD, 128), f32),
        ],
        compiler_params=pltpu.CompilerParams(vmem_limit_bytes=48 * 1024 * 1024),
        cost_estimate=pl.CostEstimate(
            flops=2 * 4096 * 8192 * 256, bytes_accessed=8 << 20, transcendentals=0
        ),
    )(where, wanted, own, other, panels)


def parts_of(value, count):
    found = []
    for _ in range(count):
        part = value.astype(bf16)
        found.append(part)
        value = value - part.astype(f32)
    return found


def refit_kernel(where, total, shared, held, out, normed, scaled, inverse):
    y = where[2]
    scaling = total[0, 161:162, :] + EPSILON
    a = lax.broadcasted_iota(jnp.int32, (128, 128), 0)
    b = lax.broadcasted_iota(jnp.int32, (128, 128), 1)
    for q in range(NX):
        sums = total[q]
        diagonal = sums[160:161, :] / scaling + DAMPING
        high, low = parts_of(sums[0:128, :] / scaling / diagonal, 2)
        at = slice(q * 128, (q + 1) * 128)
        scaled[0:128, at] = high
        scaled[128:256, at] = low
        scaled[256:384, at] = high
        rows = lax.broadcasted_iota(jnp.int32, (32, 128), 0) + q * 32
        lanes = lax.broadcasted_iota(jnp.int32, (32, 128), 1)
        damped = sums[128:160, :] / scaling + jnp.where(rows == lanes, DAMPING, 0.0)
        for k, part in enumerate(parts_of(damped, 3)):
            normed[k * 128 + q * 32 : k * 128 + q * 32 + 32, :] = part
    for q in range(NY):
        part = [shared[q, 240 + 16 * k : 256 + 16 * k, :] for k in range(3)]
        for k, source in enumerate((0, 1, 0, 2, 1, 0)):
            inverse[k * 128 + q * 16 : k * 128 + q * 16 + 16, :] = part[source]

    @pl.loop(0, NY)
    def _(q):
        numbers = shared[q, 192:240, :]
        spread = []
        for part in range(4):
            pick = jnp.where(a == part * 32 + b // 4, 1.0, 0.0).astype(bf16)
            spread.append(jnp.dot(numbers, pick, preferred_element_type=f32))
        number = jnp.concatenate(spread, axis=0)
        lane = lax.broadcasted_iota(jnp.int32, (192, 128), 1) % 4
        code = number.astype(jnp.int32)
        kept = jnp.where(lane == 0, 0b000111, jnp.where(lane == 1, 0b011001, jnp.where(lane == 2, 0b101010, 0b110100)))
        mask = ((kept >> code) & 1).astype(f32)
        panel = shared[q, 0:192, :].astype(f32)
        dropped = ((1.0 - mask) * panel).astype(bf16)
        step = jnp.dot(jnp.concatenate([dropped] * 3, axis=1), normed[...], preferred_element_type=f32)
        high, middle, low = parts_of(step, 3)
        step = jnp.dot(
            jnp.concatenate([high, high, middle, high, middle, low], axis=1),
            inverse[...],
            preferred_element_type=f32,
        )
        refitted = mask * (panel + step)
        high, low = parts_of(refitted - panel, 2)
        correction = jnp.dot(
            jnp.concatenate([high, high, low], axis=1), scaled[...], preferred_element_type=f32
        )
        for k in range(4):
            for half in range(2):
                piece = held[16 * k + 2 * q + half, 0:96, :].astype(f32)
                fixed = piece - correction[half * 96 : (half + 1) * 96, k * 128 : (k + 1) * 128]
                out[pl.ds(pl.multiple_of(q * 192 + half * 96, 32), 96), k * 128 : (k + 1) * 128] = fixed.astype(bf16)

        @pl.when(y == 0)
        def _():
            out[pl.ds(pl.multiple_of(q * 192, 64), 192), 0:128] = refitted.astype(bf16)


def refit(where, sums, shared, held):
    return pl.pallas_call(
        refit_kernel,
        out_shape=jax.ShapeDtypeStruct((FF, 512), bf16),
        in_specs=[SMEM] + [VMEM] * 3,
        out_specs=VMEM,
        scratch_shapes=[
            pltpu.VMEM((384, 128), bf16),
            pltpu.VMEM((384, 512), bf16),
            pltpu.VMEM((768, 128), bf16),
        ],
        compiler_params=pltpu.CompilerParams(vmem_limit_bytes=32 * 1024 * 1024),
    )(where, sums, shared, held)


def swap(value, axis, size, step):
    return lax.ppermute(value, axis, [(i, (i + step) % size) for i in range(size)])


def after(value, *others):
    return lax.optimization_barrier((value, *others))[0]


def shards(tokens, routes, old_slots, new_slots, weights, patterns, inverse):
    x, y, z, c = (lax.axis_index(name) for name in ("x", "y", "z", "c"))
    me = (x * NZ + z) * NC + c
    where = jnp.stack([x, c, y]).astype(jnp.int32)
    slot = jnp.arange(64, dtype=jnp.int32)
    source = jnp.sum(jnp.where(old_slots[None, :] == new_slots[:, None], slot[None, :], 0), axis=1)
    order = new_slots.reshape(NX, NZ, NC).transpose(2, 1, 0).reshape(NC, HELD)
    wanted = jnp.broadcast_to(
        lax.dynamic_index_in_dim(order, c, 0, keepdims=False)[:, None], (HELD, 128)
    ).astype(f32)

    pieces = pack(
        weights[0],
        lax.dynamic_slice_in_dim(patterns[0], y * 192, 192, 0),
        lax.dynamic_slice_in_dim(inverse[0], y * 16, 16, 0),
    )
    spread = lax.all_to_all(pieces, EXPERT, 0, 0, tiled=True)
    blocks, panel = prepare(tokens, routes)
    came = [panel] + [swap(panel, "y", NY, step) for step in range(1, NY)]
    spread, *came = lax.optimization_barrier((spread, *came))
    panels = lax.all_gather(join(came), ("x", "c"), axis=0, tiled=False).reshape(64, 144, 128)
    own = lax.all_to_all(after(blocks, spread), ("y", "x"), 0, 0, tiled=True)
    other = swap(own, "c", NC, 1)
    spread = jnp.take(spread, source, axis=0, mode="clip")
    held = lax.all_to_all(after(spread, own), EXPERT, 0, 0, tiled=True)

    sums = gram(where, wanted, own, other, panels)
    sums = lax.psum_scatter(after(sums, held), "z", scatter_dimension=0, tiled=True)
    moved = held[0:16, 0:96].reshape(NY, 192, 128)
    moved = lax.all_to_all(moved, "y", 0, 0, tiled=True)[0]
    shared = jnp.concatenate([moved, held[:, 96:98].reshape(128, 128)[0:96]], axis=0)
    shared = lax.all_gather(shared, "y", axis=0, tiled=False)
    sums = lax.all_to_all(after(sums, shared), "x", 0, 0, tiled=True)
    return refit(where, sums, shared, held)[None]


def solution(mesh):
    grid = Mesh(mesh.devices.reshape(NY, NX, NZ, NC), ("y", "x", "z", "c"))
    placed = (
        P(("y", "x", "z", "c"), None),
        P(("y", "x", "z", "c"), None),
        P(),
        P(),
        P(EXPERT, None, "y"),
        P(EXPERT, None, None),
        P(EXPERT, None, None),
    )
    return jax.shard_map(
        shards, mesh=grid, in_specs=placed, out_specs=P(EXPERT, None, "y"), check_vma=False
    )
```
